32 devices in a mesh: space: 16 (over z, y, core), cuts: 2 (over x).
Axes of the slice: x: 2, y: 2, z: 4, core: 2. Of those that a mesh axis runs over, the one named last changes fastest.
Arguments:
- vectors: float32 [2, 2, 512, 4096], P('cuts', None, None, 'space'), may hold values from -1.25 to 1.25
- momenta: int32 [3, 3], replicated, may hold values from -3 to 3, as said below
- diagrams: int32 [64, 5], replicated, may hold values from 0 to 3, as said below
Outputs:
- meson: float32 [2, 1536, 1024], P('cuts', 'space')
- diagram_values: float32 [64, 2], replicated
The draws below stay inside these ranges and needn't reach their ends.
Inputs may be any that keep to these rules, and one draw needn't show every extreme that they name: `momenta`: first component of each momentum is nonzero. `diagrams`: column 0 is a tile id below (2)**2, columns 1 and 2 are time slices, column 3 a phase, column 4 the owner index along cuts; no owner is named more than 32 times and one owner exactly 32 times.
All inputs are finite; a program needn't handle non-finite values.
Results may differ from the reference program's by a relative error of at most 0.0003.
Values sent between devices are 32-bit elements; how exact they have to be, the bound alone decides.
No kernel may reach another device: no remote copies, remote signals or barrier semaphores. Data moves between devices by JAX's collectives and lax.ppermute only.
A program may use at most 64 MiB of HBM per device.

```python
import math
import jax
import jax.numpy as jnp
from jax import lax

MODES = 512
TILE = 256
PHASES = 3
EXTENT = 96
PRODUCTS = 64
OWN_MOST = 32
SPACE_SITES = 4096
TSLICES = 2


def draw_momenta(key, part):
    keys = jax.random.split(jax.random.fold_in(key, 11), 3)
    position = jnp.arange(PHASES, dtype=jnp.int32)
    magnitude = jax.random.randint(keys[0], (PHASES,), 1, 4)
    magnitude = jnp.where(position < 2, 3, magnitude)
    signs = 2 * jax.random.randint(keys[1], (PHASES,), 0, 2) - 1
    signs = jnp.where(position == 0, 1, jnp.where(position == 1, -1, signs))
    others = jax.random.randint(keys[2], (PHASES, 2), -3, 4)
    return jnp.concatenate([(magnitude * signs)[:, None], others], axis=1).astype(jnp.int32)


def draw_diagrams(key, part):
    keys = jax.random.split(jax.random.fold_in(key, 23), 7)
    tiles = jax.random.randint(keys[0], (PRODUCTS,), 0, MODES // TILE * (MODES // TILE))
    first = jax.random.randint(keys[1], (PRODUCTS,), 0, TSLICES)
    second = jax.random.randint(keys[2], (PRODUCTS,), 0, TSLICES)
    phase = jax.random.randint(keys[3], (PRODUCTS,), 0, PHASES)
    heavy = jax.random.randint(keys[4], (), 0, TSLICES)
    others = (heavy + 1 + jax.random.randint(keys[5], (PRODUCTS,), 0, TSLICES - 1)) % TSLICES
    owner = jnp.where(jnp.arange(PRODUCTS) < OWN_MOST, heavy, others)
    order = jax.random.permutation(keys[6], PRODUCTS)
    owner = owner[order]
    return jnp.stack([tiles, first, second, phase, owner], axis=1).astype(jnp.int32)


def shard_levels(rng, shape, pieces, smallest, top_value):
    gain, own = 1.0, jax.random.fold_in(rng, 6)
    for axis_at, shards_of in pieces:
        draws = jnp.exp(jax.random.uniform(jax.random.fold_in(own, axis_at), (shards_of,), jnp.float32, smallest / len(pieces), top_value / len(pieces)))
        gain = gain * jnp.repeat(draws, shape[axis_at] // shards_of).reshape([-1 if axis == axis_at else 1 for axis in range(len(shape))])
    return gain


def gaussian(stream_key, extent, scale, limit, cuts=(), held_as=jnp.bfloat16):
    gain = shard_levels(stream_key, extent, cuts, -0.22, 0.18) if cuts else 1.0
    array = jax.random.normal(stream_key, extent, jnp.float32) * scale * gain
    return jnp.minimum(jnp.maximum(array, -limit), limit).astype(held_as)


def setup_inputs(seed: int = 0) -> dict:
    arg_keys = jax.random.split(jax.random.key(seed), 4)
    vectors = gaussian(arg_keys[0], (TSLICES, 2, MODES, SPACE_SITES), ((4 * SPACE_SITES) ** -0.25), 1.25, ((0, 2), (3, 16)), jnp.float32)
    momenta = draw_momenta(jax.random.fold_in(arg_keys[3], 71), 0)
    diagrams = draw_diagrams(jax.random.fold_in(arg_keys[3], 71), 0)
    return dict(vectors=vectors, momenta=momenta, diagrams=diagrams)


full_turn = 2.0 * math.pi


def angles_for(moment_rows, site_ids):
    coord_x = site_ids % EXTENT
    coord_y = (site_ids // EXTENT) % EXTENT
    coord_z = site_ids // (EXTENT * EXTENT)
    dotted = moment_rows[:, 0:1] * coord_x[None, :] + moment_rows[:, 1:2] * coord_y[None, :] + moment_rows[:, 2:3] * coord_z[None, :]
    return jnp.mod(dotted, EXTENT).astype(jnp.float32) * (full_turn / EXTENT)


def phased_rows(real_vec, imag_vec, moment_rows, site_ids):
    angle = angles_for(moment_rows, site_ids)
    cosine = jnp.cos(angle)
    sine = jnp.sin(angle)
    left_real = real_vec * cosine + imag_vec * sine
    left_imag = real_vec * sine - imag_vec * cosine
    return jnp.concatenate([left_real, left_imag], axis=1)


def right_block(real_vec, imag_vec):
    upper = jnp.concatenate([real_vec, -imag_vec], axis=1)
    lower = jnp.concatenate([imag_vec, real_vec], axis=1)
    return jnp.concatenate([upper, lower], axis=0)


def contract(left, right):
    return lax.dot_general(left, right, (((1,), (1,)), ((), ())), precision=lax.Precision.HIGHEST, preferred_element_type=jnp.float32)


def tile_columns(rows, column_start):
    real_cols = lax.dynamic_slice_in_dim(rows, column_start, TILE, 1)
    imag_cols = lax.dynamic_slice_in_dim(rows, column_start + MODES, TILE, 1)
    return real_cols, imag_cols


def tile_pair(first_real, first_imag, second_real, second_imag, mask):
    real_rows = jnp.sum(first_real * second_real + first_imag * second_imag, axis=1)
    imag_rows = jnp.sum(first_imag * second_real - first_real * second_imag, axis=1)
    return jnp.stack([jnp.sum(mask * real_rows), jnp.sum(mask * imag_rows)]) / TILE


def reference(vectors, momenta, diagrams):
    site_ids = jnp.arange(SPACE_SITES, dtype=jnp.int32)
    fields = []
    for slice_index in range(TSLICES):
        real_vec = vectors[slice_index, 0]
        imag_vec = vectors[slice_index, 1]
        right = right_block(real_vec, imag_vec)
        blocks = []
        for phase in range(PHASES):
            left = phased_rows(real_vec, imag_vec, momenta[phase:phase + 1], site_ids)
            blocks.append(contract(left, right))
        fields.append(jnp.concatenate(blocks, axis=0))
    meson = jnp.stack(fields)
    tiles_per = MODES // TILE

    def one_product(entry):
        tile_row = entry[0] // tiles_per
        column_start = ((entry[0] % tiles_per) * TILE).astype(jnp.int32)
        row_start = (entry[3] * MODES + tile_row * TILE).astype(jnp.int32)
        first = lax.dynamic_slice_in_dim(lax.dynamic_index_in_dim(meson, entry[1], 0, keepdims=False), row_start, TILE, 0)
        second = lax.dynamic_slice_in_dim(lax.dynamic_index_in_dim(meson, entry[2], 0, keepdims=False), row_start, TILE, 0)
        first_real, first_imag = tile_columns(first, column_start)
        second_real, second_imag = tile_columns(second, column_start)
        return tile_pair(first_real, first_imag, second_real, second_imag, jnp.ones((TILE,), jnp.float32))

    diagram_values = lax.map(one_product, diagrams)
    return meson, diagram_values
```

```python
import functools
import math

import jax
import jax.numpy as jnp
from jax import lax
from jax.experimental import pallas as pl
from jax.experimental.pallas import tpu as pltpu
from jax.sharding import PartitionSpec as P

MODES = 512
TILE = 256
PHASES = 3
EXTENT = 96

full_turn = 2.0 * math.pi
tiles_per = MODES // TILE
VMEM_LIMIT = 48 * 1024 * 1024


def angles_for(moment_rows, site_ids):
    coord_x = site_ids % EXTENT
    coord_y = site_ids // EXTENT % EXTENT
    coord_z = site_ids // (EXTENT * EXTENT)
    dotted = (
        moment_rows[:, 0:1] * coord_x[None, :]
        + moment_rows[:, 1:2] * coord_y[None, :]
        + moment_rows[:, 2:3] * coord_z[None, :]
    )
    return jnp.mod(dotted, EXTENT).astype(jnp.float32) * (full_turn / EXTENT)


def phased_rows(real_vec, imag_vec, moment_rows, site_ids):
    angle = angles_for(moment_rows, site_ids)
    cosine = jnp.cos(angle)
    sine = jnp.sin(angle)
    left_real = real_vec * cosine + imag_vec * sine
    left_imag = real_vec * sine - imag_vec * cosine
    return jnp.concatenate([left_real, left_imag], axis=1)


def right_block(real_vec, imag_vec):
    upper = jnp.concatenate([real_vec, -imag_vec], axis=1)
    lower = jnp.concatenate([imag_vec, real_vec], axis=1)
    return jnp.concatenate([upper, lower], axis=0)


def general(vectors, momenta, diagrams):
    real_vec = vectors[0, 0]
    imag_vec = vectors[0, 1]
    sites_dev = real_vec.shape[1]
    site_ids = lax.axis_index("space") * sites_dev + jnp.arange(sites_dev, dtype=jnp.int32)
    right = right_block(real_vec, imag_vec)
    own_rows = PHASES * MODES // lax.axis_size("space")
    left = jnp.concatenate(
        [phased_rows(real_vec, imag_vec, momenta[p : p + 1], site_ids) for p in range(PHASES)], axis=0
    )
    sums = lax.dot_general(
        left,
        right,
        (((1,), (1,)), ((), ())),
        precision=lax.Precision.HIGHEST,
        preferred_element_type=jnp.float32,
    )
    field_rows = lax.psum_scatter(sums, "space", scatter_dimension=0, tiled=True)
    slices = lax.all_gather(field_rows[None], "cuts", axis=0, tiled=True)
    count = slices.shape[0]
    group = (lax.axis_index("space") * own_rows + jnp.arange(own_rows, dtype=jnp.int32)) // TILE
    member = (group[None, :] == jnp.arange(PHASES * tiles_per)[:, None]).astype(jnp.float32)
    split = slices.reshape(count, own_rows, 2, tiles_per, TILE)
    real, imag = split[:, :, 0], split[:, :, 1]
    first_real, second_real = real[:, None], real[None, :]
    first_imag, second_imag = imag[:, None], imag[None, :]
    real_rows = jnp.sum(first_real * second_real + first_imag * second_imag, axis=-1)
    imag_rows = jnp.sum(first_imag * second_real - first_real * second_imag, axis=-1)
    rows = jnp.stack([real_rows, imag_rows])
    table = jnp.sum(rows[:, :, :, None] * member[None, None, None, :, :, None], axis=4)
    table = lax.psum(table, "space")
    tile, one, two, phase = (diagrams[:, i] for i in range(4))
    values = table[:, one, two, phase * tiles_per + tile // tiles_per, tile % tiles_per]
    return (field_rows[None], values.T / TILE)


CORE, Y, Z_NEAR, Z_FAR = 1, 2, 4, 8
CHUNKS = (24, 24, 24, 24)


def swap(array, bit):
    count = lax.axis_size("space")
    return lax.ppermute(array, "space", [(i, i ^ bit) for i in range(count)])


def split_kernel(own_ref, other_ref, high_ref, low_ref):
    sites = own_ref.shape[2]
    for part in range(2):
        for source, ref in enumerate((own_ref, other_ref)):
            value = ref[part]
            high = value.astype(jnp.bfloat16)
            low = (value - high.astype(jnp.float32)).astype(jnp.bfloat16)
            at = (2 * part + source) * sites
            high_ref[:, at : at + sites] = high
            low_ref[:, at : at + sites] = low


def rows_kernel(offset, rows, own_rows, own_ref, other_ref, cos_ref, sin_ref, high_ref, low_ref, send_ref, keep_ref, left_ref):
    me = lax.axis_index("space")
    sites = own_ref.shape[2]
    at = 0
    for dy in (Y, 0):
        for dn in (Z_NEAR, 0):
            for df in (Z_FAR, 0):
                block = me ^ (dy + dn + df)
                for group in range(rows // 8):
                    start = block * own_rows + (offset + 8 * group)
                    phase = start // MODES
                    mode = pl.multiple_of(start - phase * MODES, 8)
                    for source, ref in enumerate((own_ref, other_ref)):
                        real = ref[0, pl.ds(mode, 8), :]
                        imag = ref[1, pl.ds(mode, 8), :]
                        cosine = cos_ref[pl.ds(phase, 1), source * sites : (source + 1) * sites]
                        sine = sin_ref[pl.ds(phase, 1), source * sites : (source + 1) * sites]
                        left_ref[0, at : at + 8, source * sites : (source + 1) * sites] = real * cosine + imag * sine
                        left_ref[1, at : at + 8, source * sites : (source + 1) * sites] = real * sine - imag * cosine
                    at += 8
    half = at // 2
    for out_ref, begin in ((send_ref, 0), (keep_ref, half)):
        real = left_ref[0, begin : begin + half, :]
        imag = left_ref[1, begin : begin + half, :]
        real_high = real.astype(jnp.bfloat16)
        imag_high = imag.astype(jnp.bfloat16)
        real_low = (real - real_high.astype(jnp.float32)).astype(jnp.bfloat16)
        imag_low = (imag - imag_high.astype(jnp.float32)).astype(jnp.bfloat16)
        for column, parts in (
            (0, ((real_high, -imag_high), (real_low, -imag_low))),
            (1, ((imag_high, real_high), (imag_low, real_low))),
        ):
            high = jnp.concatenate(parts[0], axis=1)
            low = jnp.concatenate(parts[1], axis=1)

            def dot(a, b):
                return lax.dot_general(a, b, (((1,), (1,)), ((), ())), preferred_element_type=jnp.float32)

            out_ref[:, column * MODES : (column + 1) * MODES] = (
                dot(high, low_ref[...]) + dot(low, high_ref[...]) + dot(high, high_ref[...])
            )


def table_kernel(offset, own_rows, own_ref, other_ref, before_ref, table_ref):
    rows = own_ref.shape[0]
    first_row = lax.axis_index("space") * own_rows
    slice_index = lax.axis_index("cuts")
    first_group = first_row // TILE
    totals = [None, None]
    for at in range(0, rows, 8):
        entries = []
        for column in range(tiles_per):
            begin = column * TILE

            def cut(ref, start):
                return ref[at : at + 8, start : start + TILE]

            pairs = [(cut(own_ref, b), cut(other_ref, b)) for b in (begin, begin + MODES)]
            (real0, real1), (imag0, imag1) = [
                (jnp.where(slice_index == 0, a, b), jnp.where(slice_index == 0, b, a)) for a, b in pairs
            ]
            entries += [
                real0 * real0 + imag0 * imag0,
                real1 * real1 + imag1 * imag1,
                real0 * real1 + imag0 * imag1,
                imag0 * real1 - real0 * imag1,
            ]
        sums = jnp.concatenate(
            [jnp.sum(e[:, :128] + e[:, 128:], axis=0, keepdims=True) for e in entries], axis=0
        )
        local = (first_row + (offset + at)) // TILE - first_group
        for which in range(2):
            part = jnp.where(local == which, sums, 0.0)
            totals[which] = part if totals[which] is None else totals[which] + part
    lane = lax.broadcasted_iota(jnp.int32, (8, 128), 1)
    table = before_ref[...]
    for which in range(2):
        entry = jnp.sum(totals[which], axis=1, keepdims=True)
        entry = jnp.broadcast_to(entry, (8, 128))
        table = table + jnp.where(lane == first_group + which, entry, 0.0)
    table_ref[...] = table


def compiler_params():
    return pltpu.CompilerParams(vmem_limit_bytes=VMEM_LIMIT)


def in_vmem(count):
    return [pl.BlockSpec(memory_space=pltpu.VMEM)] * count


def halving(vectors, momenta, diagrams):
    own = vectors[0]
    sites = own.shape[2]
    me = lax.axis_index("space")
    own_rows = PHASES * MODES // lax.axis_size("space")
    within = jnp.arange(sites, dtype=jnp.int32)
    site_ids = jnp.concatenate([me * sites + within, (me ^ CORE) * sites + within])
    angle = angles_for(momenta, site_ids)
    cosine, sine = jnp.cos(angle), jnp.sin(angle)
    other = swap(own, CORE)
    high, low = pl.pallas_call(
        split_kernel,
        out_shape=[jax.ShapeDtypeStruct((MODES, 4 * sites), jnp.bfloat16)] * 2,
        in_specs=in_vmem(2),
        out_specs=in_vmem(2),
        compiler_params=compiler_params(),
        name="split",
    )(own, other)
    finished, table, offset = [], jnp.zeros((8, 128), jnp.float32), 0
    for rows in CHUNKS:
        depth = 4 * rows
        send, keep = pl.pallas_call(
            functools.partial(rows_kernel, offset, rows, own_rows),
            out_shape=[jax.ShapeDtypeStruct((depth, 2 * MODES), jnp.float32)] * 2,
            in_specs=in_vmem(6),
            out_specs=in_vmem(2),
            scratch_shapes=[pltpu.VMEM((2, 2 * depth, 2 * sites), jnp.float32)],
            compiler_params=compiler_params(),
            cost_estimate=pl.CostEstimate(
                flops=2 * 3 * 2 * depth * 2 * MODES * 4 * sites, bytes_accessed=4 * 1024 * 1024, transcendentals=0
            ),
            name="rows",
        )(own, other, cosine, sine, high, low)
        for bit in (Y, Z_NEAR, Z_FAR):
            came = swap(send, bit)
            if bit == Z_FAR:
                done = keep + came
            else:
                depth //= 2
                send = keep[:depth] + came[:depth]
                keep = keep[depth:] + came[depth:]
        across = lax.ppermute(done, "cuts", [(0, 1), (1, 0)])
        table = pl.pallas_call(
            functools.partial(table_kernel, offset, own_rows),
            out_shape=jax.ShapeDtypeStruct((8, 128), jnp.float32),
            in_specs=in_vmem(3),
            out_specs=in_vmem(1)[0],
            compiler_params=compiler_params(),
            name="table",
        )(done, across, table)
        finished.append(done)
        offset += rows
    for bit in (CORE, Y, Z_NEAR, Z_FAR):
        table = table + swap(table, bit)
    values = look_up(table, diagrams)
    return (jnp.concatenate(finished, axis=0)[None], values)


def look_up(table, diagrams):
    tile, one, two, phase = (diagrams[:, i : i + 1] for i in range(4))
    group = phase * tiles_per + tile // tiles_per
    column = tile % tiles_per
    lane = jnp.arange(128, dtype=jnp.int32)[None, :]
    picked = jnp.sum(jnp.where((lane == group)[:, None, :], table[None], 0.0), axis=2)
    kind = jnp.arange(8, dtype=jnp.int32)[None, :] - 4 * column
    same = one == two
    real = jnp.sum(jnp.where(kind == jnp.where(same, one, 2), picked, 0.0), axis=1)
    imag = jnp.sum(jnp.where((kind == 3) & ~same, picked, 0.0), axis=1)
    imag = jnp.where(one[:, 0] == 0, imag, -imag)
    return jnp.stack([real, imag], axis=1) / TILE


def solution(mesh):
    by_halves = mesh.shape["space"] == 16 and mesh.shape["cuts"] == 2
    placed = (P("cuts", None, None, "space"), P(), P())
    return jax.shard_map(
        halving if by_halves else general,
        mesh=mesh,
        in_specs=placed,
        out_specs=(P("cuts", "space", None), P()),
        check_vma=False,
    )
```

```python
import functools
import math

import jax
import jax.numpy as jnp
from jax import lax
from jax.experimental import pallas as pl
from jax.experimental.pallas import tpu as pltpu
from jax.sharding import PartitionSpec as P

MODES = 512
TILE = 256
PHASES = 3
EXTENT = 96

full_turn = 2.0 * math.pi
tiles_per = MODES // TILE
VMEM_LIMIT = 48 * 1024 * 1024


def angles_for(moment_rows, site_ids):
    coord_x = site_ids % EXTENT
    coord_y = site_ids // EXTENT % EXTENT
    coord_z = site_ids // (EXTENT * EXTENT)
    dotted = (
        moment_rows[:, 0:1] * coord_x[None, :]
        + moment_rows[:, 1:2] * coord_y[None, :]
        + moment_rows[:, 2:3] * coord_z[None, :]
    )
    return jnp.mod(dotted, EXTENT).astype(jnp.float32) * (full_turn / EXTENT)


def phased_rows(real_vec, imag_vec, moment_rows, site_ids):
    angle = angles_for(moment_rows, site_ids)
    cosine = jnp.cos(angle)
    sine = jnp.sin(angle)
    left_real = real_vec * cosine + imag_vec * sine
    left_imag = real_vec * sine - imag_vec * cosine
    return jnp.concatenate([left_real, left_imag], axis=1)


def right_block(real_vec, imag_vec):
    upper = jnp.concatenate([real_vec, -imag_vec], axis=1)
    lower = jnp.concatenate([imag_vec, real_vec], axis=1)
    return jnp.concatenate([upper, lower], axis=0)


def general(vectors, momenta, diagrams):
    real_vec = vectors[0, 0]
    imag_vec = vectors[0, 1]
    sites_dev = real_vec.shape[1]
    site_ids = lax.axis_index("space") * sites_dev + jnp.arange(sites_dev, dtype=jnp.int32)
    right = right_block(real_vec, imag_vec)
    own_rows = PHASES * MODES // lax.axis_size("space")
    left = jnp.concatenate(
        [phased_rows(real_vec, imag_vec, momenta[p : p + 1], site_ids) for p in range(PHASES)], axis=0
    )
    sums = lax.dot_general(
        left,
        right,
        (((1,), (1,)), ((), ())),
        precision=lax.Precision.HIGHEST,
        preferred_element_type=jnp.float32,
    )
    field_rows = lax.psum_scatter(sums, "space", scatter_dimension=0, tiled=True)
    slices = lax.all_gather(field_rows[None], "cuts", axis=0, tiled=True)
    count = slices.shape[0]
    group = (lax.axis_index("space") * own_rows + jnp.arange(own_rows, dtype=jnp.int32)) // TILE
    member = (group[None, :] == jnp.arange(PHASES * tiles_per)[:, None]).astype(jnp.float32)
    split = slices.reshape(count, own_rows, 2, tiles_per, TILE)
    real, imag = split[:, :, 0], split[:, :, 1]
    first_real, second_real = real[:, None], real[None, :]
    first_imag, second_imag = imag[:, None], imag[None, :]
    real_rows = jnp.sum(first_real * second_real + first_imag * second_imag, axis=-1)
    imag_rows = jnp.sum(first_imag * second_real - first_real * second_imag, axis=-1)
    rows = jnp.stack([real_rows, imag_rows])
    table = jnp.sum(rows[:, :, :, None] * member[None, None, None, :, :, None], axis=4)
    table = lax.psum(table, "space")
    tile, one, two, phase = (diagrams[:, i] for i in range(4))
    values = table[:, one, two, phase * tiles_per + tile // tiles_per, tile % tiles_per]
    return (field_rows[None], values.T / TILE)


CORE, Y, Z_NEAR, Z_FAR = 1, 2, 4, 8
STEPS = ((Y, Z_NEAR), (Z_NEAR, Y), (Z_FAR | Z_NEAR, Z_FAR | Z_NEAR))
CHUNKS = (24, 40, 32)


def swap(array, masks):
    count = lax.axis_size("space")
    return lax.ppermute(array, "space", [(i, i ^ masks[i % 2]) for i in range(count)])


def split_kernel(own_ref, other_ref, high_ref, low_ref):
    sites = own_ref.shape[2]
    for part in range(2):
        for source, ref in enumerate((own_ref, other_ref)):
            value = ref[part]
            high = value.astype(jnp.bfloat16)
            low = (value - high.astype(jnp.float32)).astype(jnp.bfloat16)
            at = (2 * part + source) * sites
            high_ref[:, at : at + sites] = high
            low_ref[:, at : at + sites] = low


def rows_kernel(offset, rows, own_rows, own_ref, other_ref, cos_ref, sin_ref, high_ref, low_ref, send_ref, keep_ref, left_ref):
    me = lax.axis_index("space")
    sites = own_ref.shape[2]
    masks = [jnp.where(me % 2 == 0, even, odd) for even, odd in STEPS]
    at = 0
    for one in (masks[0], 0):
        for two in (masks[1], 0):
            for three in (masks[2], 0):
                block = me ^ one ^ two ^ three
                for group in range(rows // 8):
                    start = block * own_rows + (offset + 8 * group)
                    phase = start // MODES
                    mode = pl.multiple_of(start - phase * MODES, 8)
                    for source, ref in enumerate((own_ref, other_ref)):
                        real = ref[0, pl.ds(mode, 8), :]
                        imag = ref[1, pl.ds(mode, 8), :]
                        cosine = cos_ref[pl.ds(phase, 1), source * sites : (source + 1) * sites]
                        sine = sin_ref[pl.ds(phase, 1), source * sites : (source + 1) * sites]
                        left_ref[0, at : at + 8, source * sites : (source + 1) * sites] = real * cosine + imag * sine
                        left_ref[1, at : at + 8, source * sites : (source + 1) * sites] = real * sine - imag * cosine
                    at += 8
    real, imag = left_ref[0], left_ref[1]
    real_high, imag_high = real.astype(jnp.bfloat16), imag.astype(jnp.bfloat16)
    real_low = (real - real_high.astype(jnp.float32)).astype(jnp.bfloat16)
    imag_low = (imag - imag_high.astype(jnp.float32)).astype(jnp.bfloat16)

    def both(real, imag):
        return jnp.concatenate(
            [jnp.concatenate([real, -imag], axis=1), jnp.concatenate([imag, real], axis=1)], axis=0
        )

    def dot(a, b):
        return lax.dot_general(a, b, (((1,), (1,)), ((), ())), preferred_element_type=jnp.float32)

    left_high, left_low = both(real_high, imag_high), both(real_low, imag_low)
    out = dot(left_high, low_ref[...]) + dot(left_low, high_ref[...]) + dot(left_high, high_ref[...])
    half = at // 2
    for column in range(2):
        columns = slice(column * MODES, (column + 1) * MODES)
        send_ref[:, columns] = out[column * at : column * at + half]
        keep_ref[:, columns] = out[column * at + half : (column + 1) * at]


def table_kernel(offset, own_rows, own_ref, other_ref, before_ref, table_ref):
    rows = own_ref.shape[0]
    first_row = lax.axis_index("space") * own_rows
    slice_index = lax.axis_index("cuts")
    first_group = first_row // TILE
    totals = [None, None]
    for at in range(0, rows, 8):
        entries = []
        for column in range(tiles_per):
            begin = column * TILE

            def cut(ref, start):
                return ref[at : at + 8, start : start + TILE]

            pairs = [(cut(own_ref, b), cut(other_ref, b)) for b in (begin, begin + MODES)]
            (real0, real1), (imag0, imag1) = [
                (jnp.where(slice_index == 0, a, b), jnp.where(slice_index == 0, b, a)) for a, b in pairs
            ]
            entries += [
                real0 * real0 + imag0 * imag0,
                real1 * real1 + imag1 * imag1,
                real0 * real1 + imag0 * imag1,
                imag0 * real1 - real0 * imag1,
            ]
        sums = jnp.concatenate(
            [jnp.sum(e[:, :128] + e[:, 128:], axis=0, keepdims=True) for e in entries], axis=0
        )
        local = (first_row + (offset + at)) // TILE - first_group
        for which in range(2):
            part = jnp.where(local == which, sums, 0.0)
            totals[which] = part if totals[which] is None else totals[which] + part
    lane = lax.broadcasted_iota(jnp.int32, (8, 128), 1)
    table = before_ref[...]
    for which in range(2):
        entry = jnp.sum(totals[which], axis=1, keepdims=True)
        entry = jnp.broadcast_to(entry, (8, 128))
        table = table + jnp.where(lane == first_group + which, entry, 0.0)
    table_ref[...] = table


def compiler_params():
    return pltpu.CompilerParams(vmem_limit_bytes=VMEM_LIMIT)


def in_vmem(count):
    return [pl.BlockSpec(memory_space=pltpu.VMEM)] * count


def halving(vectors, momenta, diagrams):
    own = vectors[0]
    sites = own.shape[2]
    me = lax.axis_index("space")
    own_rows = PHASES * MODES // lax.axis_size("space")
    within = jnp.arange(sites, dtype=jnp.int32)
    site_ids = jnp.concatenate([me * sites + within, (me ^ CORE) * sites + within])
    angle = angles_for(momenta, site_ids)
    cosine, sine = jnp.cos(angle), jnp.sin(angle)
    other = swap(own, (CORE, CORE))
    high, low = pl.pallas_call(
        split_kernel,
        out_shape=[jax.ShapeDtypeStruct((MODES, 4 * sites), jnp.bfloat16)] * 2,
        in_specs=in_vmem(2),
        out_specs=in_vmem(2),
        compiler_params=compiler_params(),
        name="split",
    )(own, other)
    finished, table, offset = [], jnp.zeros((8, 128), jnp.float32), 0
    for rows in CHUNKS:
        depth = 4 * rows
        send, keep = pl.pallas_call(
            functools.partial(rows_kernel, offset, rows, own_rows),
            out_shape=[jax.ShapeDtypeStruct((depth, 2 * MODES), jnp.float32)] * 2,
            in_specs=in_vmem(6),
            out_specs=in_vmem(2),
            scratch_shapes=[pltpu.VMEM((2, 2 * depth, 2 * sites), jnp.float32)],
            compiler_params=compiler_params(),
            cost_estimate=pl.CostEstimate(
                flops=2 * 3 * 2 * depth * 2 * MODES * 4 * sites, bytes_accessed=4 * 1024 * 1024, transcendentals=0
            ),
            name="rows",
        )(own, other, cosine, sine, high, low)
        for masks in STEPS:
            came = swap(send, masks)
            if depth == rows:
                done = keep + came
            else:
                depth //= 2
                send = keep[:depth] + came[:depth]
                keep = keep[depth:] + came[depth:]
        across = lax.ppermute(done, "cuts", [(0, 1), (1, 0)])
        table = pl.pallas_call(
            functools.partial(table_kernel, offset, own_rows),
            out_shape=jax.ShapeDtypeStruct((8, 128), jnp.float32),
            in_specs=in_vmem(3),
            out_specs=in_vmem(1)[0],
            compiler_params=compiler_params(),
            name="table",
        )(done, across, table)
        finished.append(done)
        offset += rows
    for bit in (CORE, Y, Z_NEAR, Z_FAR):
        table = table + swap(table, (bit, bit))
    values = look_up(table, diagrams)
    return (jnp.concatenate(finished, axis=0)[None], values)


def look_up(table, diagrams):
    tile, one, two, phase = (diagrams[:, i : i + 1] for i in range(4))
    group = phase * tiles_per + tile // tiles_per
    column = tile % tiles_per
    lane = jnp.arange(128, dtype=jnp.int32)[None, :]
    picked = jnp.sum(jnp.where((lane == group)[:, None, :], table[None], 0.0), axis=2)
    kind = jnp.arange(8, dtype=jnp.int32)[None, :] - 4 * column
    same = one == two
    real = jnp.sum(jnp.where(kind == jnp.where(same, one, 2), picked, 0.0), axis=1)
    imag = jnp.sum(jnp.where((kind == 3) & ~same, picked, 0.0), axis=1)
    imag = jnp.where(one[:, 0] == 0, imag, -imag)
    return jnp.stack([real, imag], axis=1) / TILE


def solution(mesh):
    by_halves = mesh.shape["space"] == 16 and mesh.shape["cuts"] == 2
    placed = (P("cuts", None, None, "space"), P(), P())
    return jax.shard_map(
        halving if by_halves else general,
        mesh=mesh,
        in_specs=placed,
        out_specs=(P("cuts", "space", None), P()),
        check_vma=False,
    )
```

```python
import functools
import math

import jax
import jax.numpy as jnp
from jax import lax
from jax.experimental import pallas as pl
from jax.experimental.pallas import tpu as pltpu
from jax.sharding import PartitionSpec as P

MODES = 512
TILE = 256
PHASES = 3
EXTENT = 96

full_turn = 2.0 * math.pi
tiles_per = MODES // TILE
VMEM_LIMIT = 48 * 1024 * 1024


def angles_for(moment_rows, site_ids):
    coord_x = site_ids % EXTENT
    coord_y = site_ids // EXTENT % EXTENT
    coord_z = site_ids // (EXTENT * EXTENT)
    dotted = (
        moment_rows[:, 0:1] * coord_x[None, :]
        + moment_rows[:, 1:2] * coord_y[None, :]
        + moment_rows[:, 2:3] * coord_z[None, :]
    )
    return jnp.mod(dotted, EXTENT).astype(jnp.float32) * (full_turn / EXTENT)


def phased_rows(real_vec, imag_vec, moment_rows, site_ids):
    angle = angles_for(moment_rows, site_ids)
    cosine = jnp.cos(angle)
    sine = jnp.sin(angle)
    left_real = real_vec * cosine + imag_vec * sine
    left_imag = real_vec * sine - imag_vec * cosine
    return jnp.concatenate([left_real, left_imag], axis=1)


def right_block(real_vec, imag_vec):
    upper = jnp.concatenate([real_vec, -imag_vec], axis=1)
    lower = jnp.concatenate([imag_vec, real_vec], axis=1)
    return jnp.concatenate([upper, lower], axis=0)


def general(vectors, momenta, diagrams):
    real_vec = vectors[0, 0]
    imag_vec = vectors[0, 1]
    sites_dev = real_vec.shape[1]
    site_ids = lax.axis_index("space") * sites_dev + jnp.arange(sites_dev, dtype=jnp.int32)
    right = right_block(real_vec, imag_vec)
    own_rows = PHASES * MODES // lax.axis_size("space")
    left = jnp.concatenate(
        [phased_rows(real_vec, imag_vec, momenta[p : p + 1], site_ids) for p in range(PHASES)], axis=0
    )
    sums = lax.dot_general(
        left,
        right,
        (((1,), (1,)), ((), ())),
        precision=lax.Precision.HIGHEST,
        preferred_element_type=jnp.float32,
    )
    field_rows = lax.psum_scatter(sums, "space", scatter_dimension=0, tiled=True)
    slices = lax.all_gather(field_rows[None], "cuts", axis=0, tiled=True)
    count = slices.shape[0]
    group = (lax.axis_index("space") * own_rows + jnp.arange(own_rows, dtype=jnp.int32)) // TILE
    member = (group[None, :] == jnp.arange(PHASES * tiles_per)[:, None]).astype(jnp.float32)
    split = slices.reshape(count, own_rows, 2, tiles_per, TILE)
    real, imag = split[:, :, 0], split[:, :, 1]
    first_real, second_real = real[:, None], real[None, :]
    first_imag, second_imag = imag[:, None], imag[None, :]
    real_rows = jnp.sum(first_real * second_real + first_imag * second_imag, axis=-1)
    imag_rows = jnp.sum(first_imag * second_real - first_real * second_imag, axis=-1)
    rows = jnp.stack([real_rows, imag_rows])
    table = jnp.sum(rows[:, :, :, None] * member[None, None, None, :, :, None], axis=4)
    table = lax.psum(table, "space")
    tile, one, two, phase = (diagrams[:, i] for i in range(4))
    values = table[:, one, two, phase * tiles_per + tile // tiles_per, tile % tiles_per]
    return (field_rows[None], values.T / TILE)


CORE, Y, Z_NEAR, Z_FAR = 1, 2, 4, 8
FAR = (Z_FAR | Z_NEAR, Z_FAR)
STEPS = {
    "both": ((Y, Z_NEAR), (Z_NEAR, Y), FAR),
    "y": ((Y, Y), (Z_NEAR, Z_NEAR), FAR),
    "z": ((Z_NEAR, Z_NEAR), (Y, Y), FAR),
}
KINDS = ("both",) * 4
CHUNKS = (16, 32, 32, 16)
GROUPS = ((0, 1), (2,), (3,))
PLAN = (
    ("rows", 0), ("rows", 1), ("add", 0, 0), ("add", 1, 0), ("rows", 2), ("add", 0, 1), ("add", 1, 1), ("rows", 3),
    ("add", 0, 2), ("add", 2, 0), ("add", 3, 0), ("add", 1, 2), ("add", 2, 1), ("add", 3, 1), ("add", 2, 2), ("add", 3, 2),
    ("table", 0), ("table", 1), ("table", 2),
)
AFTER = {
    ("add", 1, 0): (("add", 0, 0),),
    ("rows", 2): (("add", 1, 0),),
    ("add", 1, 1): (("add", 0, 1),),
    ("rows", 3): (("add", 1, 1),),
    ("add", 2, 0): (("add", 0, 2),),
    ("add", 3, 0): (("add", 2, 0),),
    ("add", 1, 2): (("add", 3, 0),),
    ("add", 2, 1): (("add", 1, 2),),
    ("add", 3, 1): (("add", 2, 1),),
    ("add", 2, 2): (("add", 3, 1),),
    ("add", 3, 2): (("add", 2, 2),),
}


def swap(array, masks):
    count = lax.axis_size("space")
    return lax.ppermute(array, "space", [(i, i ^ masks[i % 2]) for i in range(count)])


def in_two(value):
    high = value.astype(jnp.bfloat16)
    return high, (value - high.astype(jnp.float32)).astype(jnp.bfloat16)


def split_kernel(value_ref, *refs):
    high_ref, low_ref = refs[-2:]
    sites = value_ref.shape[2]
    for part in range(2):
        columns = slice(part * sites, (part + 1) * sites)
        high_ref[:, columns], low_ref[:, columns] = in_two(value_ref[part])


def rows_kernel(offset, rows, own_rows, steps, sources, started, *refs):
    refs = list(refs)
    inputs = [tuple(refs.pop(0) for _ in range(3)) for _ in sources]
    cos_ref, sin_ref = refs.pop(0), refs.pop(0)
    before = (refs.pop(0), refs.pop(0)) if started else None
    send_ref, keep_ref, left_ref = refs
    me = lax.axis_index("space")
    masks = [jnp.where(me % 2 == 0, even, odd) for even, odd in steps]
    at = 0
    for one in (masks[0], 0):
        for two in (masks[1], 0):
            for three in (masks[2], 0):
                block = me ^ one ^ two ^ three
                for group in range(rows // 8):
                    start = block * own_rows + (offset + 8 * group)
                    phase = start // MODES
                    mode = pl.multiple_of(start - phase * MODES, 8)
                    for place, (source, (ref, _, _)) in enumerate(zip(sources, inputs)):
                        real = ref[0, pl.ds(mode, 8), :]
                        imag = ref[1, pl.ds(mode, 8), :]
                        cosine = cos_ref[source, pl.ds(phase, 1), :]
                        sine = sin_ref[source, pl.ds(phase, 1), :]
                        left_ref[2 * place, at : at + 8, :] = real * cosine + imag * sine
                        left_ref[2 * place + 1, at : at + 8, :] = real * sine - imag * cosine
                    at += 8

    def both(real, imag):
        return jnp.concatenate(
            [jnp.concatenate([real, -imag], axis=1), jnp.concatenate([imag, real], axis=1)], axis=0
        )

    def dot(a, b):
        return lax.dot_general(a, b, (((1,), (1,)), ((), ())), preferred_element_type=jnp.float32)

    out = None
    for place, (_, high_ref, low_ref) in enumerate(inputs):
        real_high, real_low = in_two(left_ref[2 * place])
        imag_high, imag_low = in_two(left_ref[2 * place + 1])
        left_high, left_low = both(real_high, imag_high), both(real_low, imag_low)
        part = dot(left_high, low_ref[...]) + dot(left_low, high_ref[...]) + dot(left_high, high_ref[...])
        out = part if out is None else out + part
    half = at // 2
    for column in range(2):
        columns = slice(column * MODES, (column + 1) * MODES)
        for place, ref in enumerate((send_ref, keep_ref)):
            part = out[column * at + place * half : column * at + (place + 1) * half]
            ref[:, columns] = part + before[place][:, columns] if started else part


def halve_kernel(keep_ref, came_ref, *refs):
    send_ref, rest_ref = refs[-2:]
    half = keep_ref.shape[0] // 2
    send_ref[...] = keep_ref[:half, :] + came_ref[:half, :]
    rest_ref[...] = keep_ref[half:, :] + came_ref[half:, :]


def finish_kernel(keep_ref, came_ref, *refs):
    out_ref = refs[-1]
    rows = keep_ref.shape[0]
    done = out_ref.shape[0] - rows
    if done:
        out_ref[:done, :] = refs[0][...]
    out_ref[done:, :] = keep_ref[...] + came_ref[...]


def table_kernel(offset, own_rows, own_ref, other_ref, before_ref, table_ref):
    rows = own_ref.shape[0]
    first_row = lax.axis_index("space") * own_rows
    slice_index = lax.axis_index("cuts")
    first_group = first_row // TILE
    totals = [None, None]
    for at in range(0, rows, 8):
        entries = []
        for column in range(tiles_per):
            begin = column * TILE

            def cut(ref, start):
                return ref[at : at + 8, start : start + TILE]

            pairs = [(cut(own_ref, b), cut(other_ref, b)) for b in (begin, begin + MODES)]
            (real0, real1), (imag0, imag1) = [
                (jnp.where(slice_index == 0, a, b), jnp.where(slice_index == 0, b, a)) for a, b in pairs
            ]
            entries += [
                real0 * real0 + imag0 * imag0,
                real1 * real1 + imag1 * imag1,
                real0 * real1 + imag0 * imag1,
                imag0 * real1 - real0 * imag1,
            ]
        sums = jnp.concatenate(
            [jnp.sum(e[:, :128] + e[:, 128:], axis=0, keepdims=True) for e in entries], axis=0
        )
        local = (first_row + (offset + at)) // TILE - first_group
        for which in range(2):
            part = jnp.where(local == which, sums, 0.0)
            totals[which] = part if totals[which] is None else totals[which] + part
    lane = lax.broadcasted_iota(jnp.int32, (8, 128), 1)
    table = before_ref[...]
    for which in range(2):
        entry = jnp.broadcast_to(jnp.sum(totals[which], axis=1, keepdims=True), (8, 128))
        table = table + jnp.where(lane == first_group + which, entry, 0.0)
    table_ref[...] = table


def look_up_kernel(table_ref, where_ref, scale_ref, values_ref):
    lanes = values_ref.shape[1]
    kind = lax.broadcasted_iota(jnp.int32, (8, lanes), 0)
    lane = jnp.broadcast_to(where_ref[0:1, :], (8, lanes))
    picked = jnp.zeros((8, lanes), jnp.float32)
    for group in range(PHASES * tiles_per):
        picked = picked + jnp.where(lane == group, table_ref[:, group : group + 1], 0.0)
    for part in range(2):
        row = jnp.sum(jnp.where(kind == where_ref[part + 1 : part + 2, :], picked, 0.0), axis=0, keepdims=True)
        values_ref[part : part + 1, :] = row * scale_ref[part : part + 1, :]


VMEM_SPEC = pl.BlockSpec(memory_space=pltpu.VMEM)
ANY_SPEC = pl.BlockSpec(memory_space=pl.ANY)
TOKEN = jax.ShapeDtypeStruct((8, 128), jnp.float32)


def kernel_call(body, name, ins, outs, tokens=(), scratch=(), flops=0):
    return pl.pallas_call(
        body,
        out_shape=outs,
        in_specs=[VMEM_SPEC] * len(ins) + [ANY_SPEC] * len(tokens),
        out_specs=[VMEM_SPEC] * len(outs),
        scratch_shapes=scratch,
        compiler_params=pltpu.CompilerParams(vmem_limit_bytes=VMEM_LIMIT),
        cost_estimate=pl.CostEstimate(flops=flops, bytes_accessed=1024 * 1024, transcendentals=0),
        name=name,
    )(*ins, *tokens)


def floats(*shape):
    return jax.ShapeDtypeStruct(shape, jnp.float32)


def halving(vectors, momenta, diagrams):
    own = vectors[0]
    sites = own.shape[2]
    me = lax.axis_index("space")
    own_rows = PHASES * MODES // lax.axis_size("space")
    within = jnp.arange(sites, dtype=jnp.int32)
    site_ids = jnp.concatenate([me * sites + within, (me ^ CORE) * sites + within])
    angle = angles_for(momenta, site_ids)
    cosine, sine = (jnp.swapaxes(f(angle).reshape(PHASES, 2, sites), 0, 1) for f in (jnp.cos, jnp.sin))
    other = swap(own, (CORE, CORE))
    halves = [jax.ShapeDtypeStruct((MODES, 2 * sites), jnp.bfloat16)] * 2
    mine = own, *kernel_call(split_kernel, "split", [own], halves, (cosine, sine))

    def products(chunk, sources, inputs, started=()):
        rows = CHUNKS[chunk]
        depth = 4 * rows
        ins = [a for i in inputs for a in i] + [cosine, sine, *started]
        return kernel_call(
            functools.partial(rows_kernel, sum(CHUNKS[:chunk]), rows, own_rows, STEPS[KINDS[chunk]], sources, bool(started)),
            "rows",
            ins,
            [floats(depth, 2 * MODES)] * 2,
            scratch=[pltpu.VMEM((2 * len(sources), 2 * depth, sites), jnp.float32)],
            flops=2 * 3 * 4 * depth * MODES * 2 * sites * len(sources),
        )

    begun = products(0, (0,), (mine,))
    theirs = other, *kernel_call(split_kernel, "split", [other], halves)
    keeps, flights, groups, tokens = {}, {}, {}, {}
    table = jnp.zeros((8, 128), jnp.float32)
    for event in PLAN:
        kind, which = event[:2]
        after = [tokens[e] for e in AFTER.get(event, ())]
        if kind == "rows":
            if which == 0:
                send, keep = products(0, (1,), (theirs,), begun)
            else:
                send, keep = products(which, (0, 1), (mine, theirs))
            keeps[which], flights[which] = keep, swap(send, STEPS[KINDS[which]][0])
        elif kind == "add" and event[2] < 2:
            keep, came = keeps[which], flights[which]
            half = keep.shape[0] // 2
            if after:
                send, keep = kernel_call(halve_kernel, "halve", [keep, came], [floats(half, 2 * MODES)] * 2, after)
            else:
                send, keep = keep[:half] + came[:half], keep[half:] + came[half:]
            tokens[event] = keep
            keeps[which], flights[which] = keep, swap(send, STEPS[KINDS[which]][event[2] + 1])
        elif kind == "add":
            group = next(g for g in GROUPS if which in g)
            keep, came = keeps[which], flights[which]
            before = [groups[group]] if group in groups else []
            if after or before:
                rows = CHUNKS[which] + sum(b.shape[0] for b in before)
                (done,) = kernel_call(finish_kernel, "finish", [keep, came, *before], [floats(rows, 2 * MODES)], after)
            else:
                done = keep + came
            tokens[event] = groups[group] = done
            if which == group[-1]:
                flights[group] = lax.ppermute(done, "cuts", [(0, 1), (1, 0)])
        else:
            group = GROUPS[which]
            (table,) = kernel_call(
                functools.partial(table_kernel, sum(CHUNKS[: group[0]]), own_rows),
                "table",
                [groups[group], flights[group], table],
                [TOKEN],
                after,
            )
    for bit in (CORE, Y, Z_NEAR, Z_FAR):
        table = table + swap(table, (bit, bit))
    tile, one, two, phase = (diagrams[:, i] for i in range(4))
    column = 4 * (tile % tiles_per)
    same = one == two
    where = jnp.stack([phase * tiles_per + tile // tiles_per, column + jnp.where(same, one, 2), column + 3])
    sign = jnp.where(same, 0.0, jnp.where(one == 0, 1.0, -1.0))
    scale = jnp.stack([jnp.ones_like(sign), sign]) / TILE
    (values,) = kernel_call(look_up_kernel, "look_up", [table, where, scale], [floats(2, diagrams.shape[0])])
    return (jnp.concatenate([groups[g] for g in GROUPS], axis=0)[None], values.T)


def solution(mesh):
    by_halves = mesh.shape["space"] == 16 and mesh.shape["cuts"] == 2
    placed = (P("cuts", None, None, "space"), P(), P())
    return jax.shard_map(
        halving if by_halves else general,
        mesh=mesh,
        in_specs=placed,
        out_specs=(P("cuts", "space", None), P()),
        check_vma=False,
    )
```

```python
import functools
import math

import jax
import jax.numpy as jnp
from jax import lax
from jax.experimental import pallas as pl
from jax.experimental.pallas import tpu as pltpu
from jax.sharding import PartitionSpec as P

MODES = 512
TILE = 256
PHASES = 3
EXTENT = 96

full_turn = 2.0 * math.pi
tiles_per = MODES // TILE
VMEM_LIMIT = 48 * 1024 * 1024


def angles_for(moment_rows, site_ids):
    coord_x = site_ids % EXTENT
    coord_y = site_ids // EXTENT % EXTENT
    coord_z = site_ids // (EXTENT * EXTENT)
    dotted = (
        moment_rows[:, 0:1] * coord_x[None, :]
        + moment_rows[:, 1:2] * coord_y[None, :]
        + moment_rows[:, 2:3] * coord_z[None, :]
    )
    return jnp.mod(dotted, EXTENT).astype(jnp.float32) * (full_turn / EXTENT)


def phased_rows(real_vec, imag_vec, moment_rows, site_ids):
    angle = angles_for(moment_rows, site_ids)
    cosine = jnp.cos(angle)
    sine = jnp.sin(angle)
    left_real = real_vec * cosine + imag_vec * sine
    left_imag = real_vec * sine - imag_vec * cosine
    return jnp.concatenate([left_real, left_imag], axis=1)


def right_block(real_vec, imag_vec):
    upper = jnp.concatenate([real_vec, -imag_vec], axis=1)
    lower = jnp.concatenate([imag_vec, real_vec], axis=1)
    return jnp.concatenate([upper, lower], axis=0)


def general(vectors, momenta, diagrams):
    real_vec = vectors[0, 0]
    imag_vec = vectors[0, 1]
    sites_dev = real_vec.shape[1]
    site_ids = lax.axis_index("space") * sites_dev + jnp.arange(sites_dev, dtype=jnp.int32)
    right = right_block(real_vec, imag_vec)
    own_rows = PHASES * MODES // lax.axis_size("space")
    left = jnp.concatenate(
        [phased_rows(real_vec, imag_vec, momenta[p : p + 1], site_ids) for p in range(PHASES)], axis=0
    )
    sums = lax.dot_general(
        left,
        right,
        (((1,), (1,)), ((), ())),
        precision=lax.Precision.HIGHEST,
        preferred_element_type=jnp.float32,
    )
    field_rows = lax.psum_scatter(sums, "space", scatter_dimension=0, tiled=True)
    slices = lax.all_gather(field_rows[None], "cuts", axis=0, tiled=True)
    count = slices.shape[0]
    group = (lax.axis_index("space") * own_rows + jnp.arange(own_rows, dtype=jnp.int32)) // TILE
    member = (group[None, :] == jnp.arange(PHASES * tiles_per)[:, None]).astype(jnp.float32)
    split = slices.reshape(count, own_rows, 2, tiles_per, TILE)
    real, imag = split[:, :, 0], split[:, :, 1]
    first_real, second_real = real[:, None], real[None, :]
    first_imag, second_imag = imag[:, None], imag[None, :]
    real_rows = jnp.sum(first_real * second_real + first_imag * second_imag, axis=-1)
    imag_rows = jnp.sum(first_imag * second_real - first_real * second_imag, axis=-1)
    rows = jnp.stack([real_rows, imag_rows])
    table = jnp.sum(rows[:, :, :, None] * member[None, None, None, :, :, None], axis=4)
    table = lax.psum(table, "space")
    tile, one, two, phase = (diagrams[:, i] for i in range(4))
    values = table[:, one, two, phase * tiles_per + tile // tiles_per, tile % tiles_per]
    return (field_rows[None], values.T / TILE)


CORE, Y, Z_NEAR, Z_FAR = 1, 2, 4, 8
STEPS = (
    ((Y, Z_NEAR), (Z_NEAR, Y), (Z_FAR | Z_NEAR, Z_FAR)),
    ((Y, Z_NEAR), (Z_NEAR, Y), (Z_FAR | Z_NEAR, Z_FAR)),
    ((Y, Z_NEAR), (Z_NEAR, Y), (Z_FAR | Z_NEAR, Z_FAR)),
    ((Y, Z_NEAR), (Z_NEAR, Y), (Z_FAR, Z_FAR)),
)
CHUNKS = (16, 32, 32, 16)
GROUPS = ((0, 1), (2,), (3,))
PLAN = (
    ("rows", 0), ("rows", 1), ("add", 0, 0), ("add", 1, 0), ("rows", 2), ("add", 0, 1), ("add", 1, 1), ("rows", 3),
    ("add", 0, 2), ("add", 2, 0), ("add", 3, 0), ("add", 1, 2), ("add", 2, 1), ("add", 3, 1), ("add", 2, 2), ("add", 3, 2),
    ("table", 0), ("table", 1), ("table", 2),
)
AFTER = {
    ("rows", 1): (("rows", 0),),
    ("add", 1, 0): (("add", 0, 0),),
    ("add", 1, 1): (("add", 0, 1),),
    ("add", 2, 0): (("add", 0, 2),),
    ("add", 3, 0): (("add", 2, 0),),
    ("add", 1, 2): (("add", 3, 0),),
    ("add", 2, 1): (("add", 1, 2),),
    ("add", 3, 1): (("add", 2, 1),),
    ("add", 2, 2): (("add", 3, 1),),
    ("add", 3, 2): (("add", 2, 2),),
}


def swap(array, masks):
    count = lax.axis_size("space")
    return lax.ppermute(array, "space", [(i, i ^ masks[i % 2]) for i in range(count)])


def in_two(value):
    high = value.astype(jnp.bfloat16)
    return high, (value - high.astype(jnp.float32)).astype(jnp.bfloat16)


def split_kernel(value_ref, high_ref, low_ref):
    sites = value_ref.shape[2]
    for part in range(2):
        columns = slice(part * sites, (part + 1) * sites)
        high_ref[:, columns], low_ref[:, columns] = in_two(value_ref[part])


def rows_kernel(offset, rows, own_rows, steps, count, *refs):
    inputs = [refs[3 * source : 3 * source + 3] for source in range(count)]
    cos_ref, sin_ref = refs[3 * count : 3 * count + 2]
    send_ref, keep_ref, left_ref = refs[-3:]
    me = lax.axis_index("space")
    masks = [jnp.where(me % 2 == 0, even, odd) for even, odd in steps]
    at = 0
    for one in (masks[0], 0):
        for two in (masks[1], 0):
            for three in (masks[2], 0):
                block = me ^ one ^ two ^ three
                for group in range(rows // 8):
                    start = block * own_rows + (offset + 8 * group)
                    phase = start // MODES
                    mode = pl.multiple_of(start - phase * MODES, 8)
                    for place, (ref, _, _) in enumerate(inputs):
                        real = ref[0, pl.ds(mode, 8), :]
                        imag = ref[1, pl.ds(mode, 8), :]
                        cosine = cos_ref[place, pl.ds(phase, 1), :]
                        sine = sin_ref[place, pl.ds(phase, 1), :]
                        left_ref[2 * place, at : at + 8, :] = real * cosine + imag * sine
                        left_ref[2 * place + 1, at : at + 8, :] = real * sine - imag * cosine
                    at += 8

    def both(real, imag):
        return jnp.concatenate(
            [jnp.concatenate([real, -imag], axis=1), jnp.concatenate([imag, real], axis=1)], axis=0
        )

    def dot(a, b):
        return lax.dot_general(a, b, (((1,), (1,)), ((), ())), preferred_element_type=jnp.float32)

    out = None
    for place, (_, high_ref, low_ref) in enumerate(inputs):
        real_high, real_low = in_two(left_ref[2 * place])
        imag_high, imag_low = in_two(left_ref[2 * place + 1])
        left_high, left_low = both(real_high, imag_high), both(real_low, imag_low)
        part = dot(left_high, low_ref[...]) + dot(left_low, high_ref[...]) + dot(left_high, high_ref[...])
        out = part if out is None else out + part
    half = at // 2
    for column in range(2):
        columns = slice(column * MODES, (column + 1) * MODES)
        for place, ref in enumerate((send_ref, keep_ref)):
            ref[:, columns] = out[column * at + place * half : column * at + (place + 1) * half]


def halve_kernel(keep_ref, came_ref, *refs):
    send_ref, rest_ref = refs[-2:]
    half = keep_ref.shape[0] // 2
    send_ref[...] = keep_ref[:half, :] + came_ref[:half, :]
    rest_ref[...] = keep_ref[half:, :] + came_ref[half:, :]


def finish_kernel(keep_ref, came_ref, *refs):
    out_ref = refs[-1]
    rows = keep_ref.shape[0]
    done = out_ref.shape[0] - rows
    if done:
        out_ref[:done, :] = refs[0][...]
    out_ref[done:, :] = keep_ref[...] + came_ref[...]


def table_kernel(offset, own_rows, own_ref, other_ref, before_ref, table_ref):
    rows = own_ref.shape[0]
    first_row = lax.axis_index("space") * own_rows
    slice_index = lax.axis_index("cuts")
    first_group = first_row // TILE
    totals = [None, None]
    for at in range(0, rows, 8):
        entries = []
        for column in range(tiles_per):
            begin = column * TILE

            def cut(ref, start):
                return ref[at : at + 8, start : start + TILE]

            pairs = [(cut(own_ref, b), cut(other_ref, b)) for b in (begin, begin + MODES)]
            (real0, real1), (imag0, imag1) = [
                (jnp.where(slice_index == 0, a, b), jnp.where(slice_index == 0, b, a)) for a, b in pairs
            ]
            entries += [
                real0 * real0 + imag0 * imag0,
                real1 * real1 + imag1 * imag1,
                real0 * real1 + imag0 * imag1,
                imag0 * real1 - real0 * imag1,
            ]
        sums = jnp.concatenate(
            [jnp.sum(e[:, :128] + e[:, 128:], axis=0, keepdims=True) for e in entries], axis=0
        )
        local = (first_row + (offset + at)) // TILE - first_group
        for which in range(2):
            part = jnp.where(local == which, sums, 0.0)
            totals[which] = part if totals[which] is None else totals[which] + part
    lane = lax.broadcasted_iota(jnp.int32, (8, 128), 1)
    table = before_ref[...]
    for which in range(2):
        entry = jnp.broadcast_to(jnp.sum(totals[which], axis=1, keepdims=True), (8, 128))
        table = table + jnp.where(lane == first_group + which, entry, 0.0)
    table_ref[...] = table


def look_up_kernel(table_ref, where_ref, scale_ref, values_ref):
    lanes = values_ref.shape[1]
    kind = lax.broadcasted_iota(jnp.int32, (8, lanes), 0)
    lane = jnp.broadcast_to(where_ref[0:1, :], (8, lanes))
    picked = jnp.zeros((8, lanes), jnp.float32)
    for group in range(PHASES * tiles_per):
        picked = picked + jnp.where(lane == group, table_ref[:, group : group + 1], 0.0)
    for part in range(2):
        row = jnp.sum(jnp.where(kind == where_ref[part + 1 : part + 2, :], picked, 0.0), axis=0, keepdims=True)
        values_ref[part : part + 1, :] = row * scale_ref[part : part + 1, :]


VMEM_SPEC = pl.BlockSpec(memory_space=pltpu.VMEM)
ANY_SPEC = pl.BlockSpec(memory_space=pl.ANY)
TOKEN = jax.ShapeDtypeStruct((8, 128), jnp.float32)


def kernel_call(body, name, ins, outs, tokens=(), scratch=(), flops=0):
    return pl.pallas_call(
        body,
        out_shape=outs,
        in_specs=[VMEM_SPEC] * len(ins) + [ANY_SPEC] * len(tokens),
        out_specs=[VMEM_SPEC] * len(outs),
        scratch_shapes=scratch,
        compiler_params=pltpu.CompilerParams(vmem_limit_bytes=VMEM_LIMIT),
        cost_estimate=pl.CostEstimate(flops=flops, bytes_accessed=1024 * 1024, transcendentals=0),
        name=name,
    )(*ins, *tokens)


def floats(*shape):
    return jax.ShapeDtypeStruct(shape, jnp.float32)


def halving(vectors, momenta, diagrams):
    own = vectors[0]
    sites = own.shape[2]
    me = lax.axis_index("space")
    own_rows = PHASES * MODES // lax.axis_size("space")
    within = jnp.arange(sites, dtype=jnp.int32)
    site_ids = jnp.concatenate([me * sites + within, (me ^ CORE) * sites + within])
    angle = angles_for(momenta, site_ids)
    cosine, sine = (jnp.swapaxes(f(angle).reshape(PHASES, 2, sites), 0, 1) for f in (jnp.cos, jnp.sin))
    other = swap(own, (CORE, CORE))
    halves = [jax.ShapeDtypeStruct((MODES, 2 * sites), jnp.bfloat16)] * 2
    mine = own, *kernel_call(split_kernel, "split", [own], halves)

    def products(chunk, inputs, after):
        rows = CHUNKS[chunk]
        depth = 4 * rows
        ins = [a for i in inputs for a in i] + [cosine, sine]
        return kernel_call(
            functools.partial(rows_kernel, sum(CHUNKS[:chunk]), rows, own_rows, STEPS[chunk], len(inputs)),
            "rows",
            ins,
            [floats(depth, 2 * MODES)] * 2,
            after,
            scratch=[pltpu.VMEM((2 * len(inputs), 2 * depth, sites), jnp.float32)],
            flops=2 * 3 * 4 * depth * MODES * 2 * sites * len(inputs),
        )

    theirs = other, *kernel_call(split_kernel, "split", [other], halves)
    keeps, flights, groups, tokens = {}, {}, {}, {}
    table = jnp.zeros((8, 128), jnp.float32)
    for event in PLAN:
        kind, which = event[:2]
        after = [tokens[e] for e in AFTER.get(event, ())]
        if kind == "rows":
            send, keep = products(which, (mine, theirs), after)
            tokens[event] = keep
            keeps[which], flights[which] = keep, swap(send, STEPS[which][0])
        elif kind == "add" and event[2] < 2:
            keep, came = keeps[which], flights[which]
            half = keep.shape[0] // 2
            if after:
                send, keep = kernel_call(halve_kernel, "halve", [keep, came], [floats(half, 2 * MODES)] * 2, after)
            else:
                send, keep = keep[:half] + came[:half], keep[half:] + came[half:]
            tokens[event] = keep
            keeps[which], flights[which] = keep, swap(send, STEPS[which][event[2] + 1])
        elif kind == "add":
            group = next(g for g in GROUPS if which in g)
            keep, came = keeps[which], flights[which]
            before = [groups[group]] if group in groups else []
            if after or before:
                rows = CHUNKS[which] + sum(b.shape[0] for b in before)
                (done,) = kernel_call(finish_kernel, "finish", [keep, came, *before], [floats(rows, 2 * MODES)], after)
            else:
                done = keep + came
            tokens[event] = groups[group] = done
            if which == group[-1]:
                flights[group] = lax.ppermute(done, "cuts", [(0, 1), (1, 0)])
        else:
            group = GROUPS[which]
            (table,) = kernel_call(
                functools.partial(table_kernel, sum(CHUNKS[: group[0]]), own_rows),
                "table",
                [groups[group], flights[group], table],
                [TOKEN],
                after,
            )
    for bit in (CORE, Z_NEAR, Y, Z_FAR):
        table = table + swap(table, (bit, bit))
    tile, one, two, phase = (diagrams[:, i] for i in range(4))
    column = 4 * (tile % tiles_per)
    same = one == two
    where = jnp.stack([phase * tiles_per + tile // tiles_per, column + jnp.where(same, one, 2), column + 3])
    sign = jnp.where(same, 0.0, jnp.where(one == 0, 1.0, -1.0))
    scale = jnp.stack([jnp.ones_like(sign), sign]) / TILE
    (values,) = kernel_call(look_up_kernel, "look_up", [table, where, scale], [floats(2, diagrams.shape[0])])
    return (jnp.concatenate([groups[g] for g in GROUPS], axis=0)[None], values.T)


def solution(mesh):
    by_halves = mesh.shape["space"] == 16 and mesh.shape["cuts"] == 2
    placed = (P("cuts", None, None, "space"), P(), P())
    return jax.shard_map(
        halving if by_halves else general,
        mesh=mesh,
        in_specs=placed,
        out_specs=(P("cuts", "space", None), P()),
        check_vma=False,
    )
```

```python
import functools
import math

import jax
import jax.numpy as jnp
from jax import lax
from jax.experimental import pallas as pl
from jax.experimental.pallas import tpu as pltpu
from jax.sharding import PartitionSpec as P

MODES = 512
TILE = 256
PHASES = 3
EXTENT = 96

full_turn = 2.0 * math.pi
tiles_per = MODES // TILE
VMEM_LIMIT = 48 * 1024 * 1024


def angles_for(moment_rows, site_ids):
    coord_x = site_ids % EXTENT
    coord_y = site_ids // EXTENT % EXTENT
    coord_z = site_ids // (EXTENT * EXTENT)
    dotted = (
        moment_rows[:, 0:1] * coord_x[None, :]
        + moment_rows[:, 1:2] * coord_y[None, :]
        + moment_rows[:, 2:3] * coord_z[None, :]
    )
    return jnp.mod(dotted, EXTENT).astype(jnp.float32) * (full_turn / EXTENT)


def phased_rows(real_vec, imag_vec, moment_rows, site_ids):
    angle = angles_for(moment_rows, site_ids)
    cosine = jnp.cos(angle)
    sine = jnp.sin(angle)
    left_real = real_vec * cosine + imag_vec * sine
    left_imag = real_vec * sine - imag_vec * cosine
    return jnp.concatenate([left_real, left_imag], axis=1)


def right_block(real_vec, imag_vec):
    upper = jnp.concatenate([real_vec, -imag_vec], axis=1)
    lower = jnp.concatenate([imag_vec, real_vec], axis=1)
    return jnp.concatenate([upper, lower], axis=0)


def general(vectors, momenta, diagrams):
    real_vec = vectors[0, 0]
    imag_vec = vectors[0, 1]
    sites_dev = real_vec.shape[1]
    site_ids = lax.axis_index("space") * sites_dev + jnp.arange(sites_dev, dtype=jnp.int32)
    right = right_block(real_vec, imag_vec)
    own_rows = PHASES * MODES // lax.axis_size("space")
    left = jnp.concatenate(
        [phased_rows(real_vec, imag_vec, momenta[p : p + 1], site_ids) for p in range(PHASES)], axis=0
    )
    sums = lax.dot_general(
        left,
        right,
        (((1,), (1,)), ((), ())),
        precision=lax.Precision.HIGHEST,
        preferred_element_type=jnp.float32,
    )
    field_rows = lax.psum_scatter(sums, "space", scatter_dimension=0, tiled=True)
    slices = lax.all_gather(field_rows[None], "cuts", axis=0, tiled=True)
    count = slices.shape[0]
    group = (lax.axis_index("space") * own_rows + jnp.arange(own_rows, dtype=jnp.int32)) // TILE
    member = (group[None, :] == jnp.arange(PHASES * tiles_per)[:, None]).astype(jnp.float32)
    split = slices.reshape(count, own_rows, 2, tiles_per, TILE)
    real, imag = split[:, :, 0], split[:, :, 1]
    first_real, second_real = real[:, None], real[None, :]
    first_imag, second_imag = imag[:, None], imag[None, :]
    real_rows = jnp.sum(first_real * second_real + first_imag * second_imag, axis=-1)
    imag_rows = jnp.sum(first_imag * second_real - first_real * second_imag, axis=-1)
    rows = jnp.stack([real_rows, imag_rows])
    table = jnp.sum(rows[:, :, :, None] * member[None, None, None, :, :, None], axis=4)
    table = lax.psum(table, "space")
    tile, one, two, phase = (diagrams[:, i] for i in range(4))
    values = table[:, one, two, phase * tiles_per + tile // tiles_per, tile % tiles_per]
    return (field_rows[None], values.T / TILE)


CORE, Y, Z_NEAR, Z_FAR = 1, 2, 4, 8
STEPS = (
    ((Y, Z_NEAR), (Z_NEAR, Y), (Z_FAR | Z_NEAR, Z_FAR)),
    ((Y, Z_NEAR), (Z_NEAR, Y), (Z_FAR | Z_NEAR, Z_FAR)),
    ((Y, Z_NEAR), (Z_NEAR, Y), (Z_FAR | Z_NEAR, Z_FAR)),
    ((Y, Z_NEAR), (Z_NEAR, Y), (Z_FAR, Z_FAR)),
)
CHUNKS = (16, 32, 32, 16)
GROUPS = ((0, 1), (2,), (3,))
PLAN = (
    ("rows", 0), ("rows", 1), ("add", 0, 0), ("add", 1, 0), ("rows", 2), ("add", 0, 1), ("add", 1, 1), ("rows", 3),
    ("add", 0, 2), ("add", 2, 0), ("add", 3, 0), ("add", 1, 2), ("add", 2, 1), ("add", 3, 1), ("add", 2, 2), ("add", 3, 2),
    ("table", 0), ("table", 1), ("table", 2),
)
AFTER = {
    ("rows", 1): (("rows", 0),),
    ("add", 1, 0): (("add", 0, 0),),
    ("add", 1, 1): (("add", 0, 1),),
    ("add", 2, 0): (("add", 0, 2),),
    ("add", 3, 0): (("add", 2, 0),),
    ("add", 1, 2): (("add", 3, 0),),
    ("add", 2, 1): (("add", 1, 2),),
    ("add", 3, 1): (("add", 2, 1),),
    ("add", 2, 2): (("add", 3, 1),),
    ("add", 3, 2): (("add", 2, 2),),
}


def swap(array, masks):
    count = lax.axis_size("space")
    return lax.ppermute(array, "space", [(i, i ^ masks[i % 2]) for i in range(count)])


def in_two(value):
    high = value.astype(jnp.bfloat16)
    return high, (value - high.astype(jnp.float32)).astype(jnp.bfloat16)


def split_kernel(value_ref, high_ref, low_ref):
    sites = value_ref.shape[2]
    for part in range(2):
        columns = slice(part * sites, (part + 1) * sites)
        high_ref[:, columns], low_ref[:, columns] = in_two(value_ref[part])


def rows_kernel(offset, rows, own_rows, steps, count, *refs):
    inputs = [refs[3 * source : 3 * source + 3] for source in range(count)]
    cos_ref, sin_ref = refs[3 * count : 3 * count + 2]
    send_ref, keep_ref, left_ref = refs[-3:]
    me = lax.axis_index("space")
    masks = [jnp.where(me % 2 == 0, even, odd) for even, odd in steps]
    at = 0
    for one in (masks[0], 0):
        for two in (masks[1], 0):
            for three in (masks[2], 0):
                block = me ^ one ^ two ^ three
                for group in range(rows // 8):
                    start = block * own_rows + (offset + 8 * group)
                    phase = start // MODES
                    mode = pl.multiple_of(start - phase * MODES, 8)
                    for place, (ref, _, _) in enumerate(inputs):
                        real = ref[0, pl.ds(mode, 8), :]
                        imag = ref[1, pl.ds(mode, 8), :]
                        cosine = cos_ref[place, pl.ds(phase, 1), :]
                        sine = sin_ref[place, pl.ds(phase, 1), :]
                        left_ref[2 * place, at : at + 8, :] = real * cosine + imag * sine
                        left_ref[2 * place + 1, at : at + 8, :] = real * sine - imag * cosine
                    at += 8

    def both(real, imag):
        return jnp.concatenate(
            [jnp.concatenate([real, -imag], axis=1), jnp.concatenate([imag, real], axis=1)], axis=0
        )

    def dot(a, b):
        return lax.dot_general(a, b, (((1,), (1,)), ((), ())), preferred_element_type=jnp.float32)

    out = None
    for place, (_, high_ref, low_ref) in enumerate(inputs):
        real_high, real_low = in_two(left_ref[2 * place])
        imag_high, imag_low = in_two(left_ref[2 * place + 1])
        left_high, left_low = both(real_high, imag_high), both(real_low, imag_low)
        part = dot(left_high, low_ref[...]) + dot(left_low, high_ref[...]) + dot(left_high, high_ref[...])
        out = part if out is None else out + part
    half = at // 2
    for column in range(2):
        columns = slice(column * MODES, (column + 1) * MODES)
        for place, ref in enumerate((send_ref, keep_ref)):
            ref[:, columns] = out[column * at + place * half : column * at + (place + 1) * half]


def halve_kernel(keep_ref, came_ref, *refs):
    send_ref, rest_ref = refs[-2:]
    half = keep_ref.shape[0] // 2
    send_ref[...] = keep_ref[:half, :] + came_ref[:half, :]
    rest_ref[...] = keep_ref[half:, :] + came_ref[half:, :]


def finish_kernel(keep_ref, came_ref, *refs):
    out_ref = refs[-1]
    rows = keep_ref.shape[0]
    done = out_ref.shape[0] - rows
    if done:
        out_ref[:done, :] = refs[0][...]
    out_ref[done:, :] = keep_ref[...] + came_ref[...]


def table_kernel(offset, own_rows, own_ref, other_ref, before_ref, table_ref):
    rows = own_ref.shape[0]
    first_row = lax.axis_index("space") * own_rows
    slice_index = lax.axis_index("cuts")
    first_group = first_row // TILE
    totals = [None, None]
    for at in range(0, rows, 8):
        entries = []
        for column in range(tiles_per):
            begin = column * TILE

            def cut(ref, start):
                return ref[at : at + 8, start : start + TILE]

            pairs = [(cut(own_ref, b), cut(other_ref, b)) for b in (begin, begin + MODES)]
            (real0, real1), (imag0, imag1) = [
                (jnp.where(slice_index == 0, a, b), jnp.where(slice_index == 0, b, a)) for a, b in pairs
            ]
            entries += [
                real0 * real0 + imag0 * imag0,
                real1 * real1 + imag1 * imag1,
                real0 * real1 + imag0 * imag1,
                imag0 * real1 - real0 * imag1,
            ]
        sums = jnp.concatenate(
            [jnp.sum(e[:, :128] + e[:, 128:], axis=0, keepdims=True) for e in entries], axis=0
        )
        local = (first_row + (offset + at)) // TILE - first_group
        for which in range(2):
            part = jnp.where(local == which, sums, 0.0)
            totals[which] = part if totals[which] is None else totals[which] + part
    lane = lax.broadcasted_iota(jnp.int32, (8, 128), 1)
    table = before_ref[...]
    for which in range(2):
        entry = jnp.broadcast_to(jnp.sum(totals[which], axis=1, keepdims=True), (8, 128))
        table = table + jnp.where(lane == first_group + which, entry, 0.0)
    table_ref[...] = table


def look_up_kernel(table_ref, where_ref, scale_ref, values_ref):
    lanes = values_ref.shape[1]
    kind = lax.broadcasted_iota(jnp.int32, (8, lanes), 0)
    lane = jnp.broadcast_to(where_ref[0:1, :], (8, lanes))
    picked = jnp.zeros((8, lanes), jnp.float32)
    for group in range(PHASES * tiles_per):
        picked = picked + jnp.where(lane == group, table_ref[:, group : group + 1], 0.0)
    for part in range(2):
        row = jnp.sum(jnp.where(kind == where_ref[part + 1 : part + 2, :], picked, 0.0), axis=0, keepdims=True)
        values_ref[part : part + 1, :] = row * scale_ref[part : part + 1, :]


VMEM_SPEC = pl.BlockSpec(memory_space=pltpu.VMEM)
ANY_SPEC = pl.BlockSpec(memory_space=pl.ANY)
TOKEN = jax.ShapeDtypeStruct((8, 128), jnp.float32)


def kernel_call(body, name, ins, outs, tokens=(), scratch=(), flops=0):
    return pl.pallas_call(
        body,
        out_shape=outs,
        in_specs=[VMEM_SPEC] * len(ins) + [ANY_SPEC] * len(tokens),
        out_specs=[VMEM_SPEC] * len(outs),
        scratch_shapes=scratch,
        compiler_params=pltpu.CompilerParams(vmem_limit_bytes=VMEM_LIMIT),
        cost_estimate=pl.CostEstimate(flops=flops, bytes_accessed=1024 * 1024, transcendentals=0),
        name=name,
    )(*ins, *tokens)


def floats(*shape):
    return jax.ShapeDtypeStruct(shape, jnp.float32)


def halving(vectors, momenta, diagrams):
    own = vectors[0]
    sites = own.shape[2]
    me = lax.axis_index("space")
    own_rows = PHASES * MODES // lax.axis_size("space")
    within = jnp.arange(sites, dtype=jnp.int32)
    site_ids = jnp.concatenate([me * sites + within, (me ^ CORE) * sites + within])
    angle = angles_for(momenta, site_ids)
    cosine, sine = (jnp.swapaxes(f(angle).reshape(PHASES, 2, sites), 0, 1) for f in (jnp.cos, jnp.sin))
    other = swap(own, (CORE, CORE))
    halves = [jax.ShapeDtypeStruct((MODES, 2 * sites), jnp.bfloat16)] * 2
    mine = own, *kernel_call(split_kernel, "split", [own], halves)

    def products(chunk, inputs, after):
        rows = CHUNKS[chunk]
        depth = 4 * rows
        ins = [a for i in inputs for a in i] + [cosine, sine]
        return kernel_call(
            functools.partial(rows_kernel, sum(CHUNKS[:chunk]), rows, own_rows, STEPS[chunk], len(inputs)),
            "rows",
            ins,
            [floats(depth, 2 * MODES)] * 2,
            after,
            scratch=[pltpu.VMEM((2 * len(inputs), 2 * depth, sites), jnp.float32)],
            flops=2 * 3 * 4 * depth * MODES * 2 * sites * len(inputs),
        )

    theirs = other, *kernel_call(split_kernel, "split", [other], halves)
    tile, one, two, phase = (diagrams[:, i] for i in range(4))
    column = 4 * (tile % tiles_per)
    same = one == two
    where = jnp.stack([phase * tiles_per + tile // tiles_per, column + jnp.where(same, one, 2), column + 3])
    sign = jnp.where(same, 0.0, jnp.where(one == 0, 1.0, -1.0))
    scale = jnp.stack([jnp.ones_like(sign), sign]) / TILE
    keeps, flights, groups, tokens = {}, {}, {}, {}
    table = jnp.zeros((8, 128), jnp.float32)
    for event in PLAN:
        kind, which = event[:2]
        after = [tokens[e] for e in AFTER.get(event, ())]
        if event == ("add", 1, 0):
            after += [where, scale]
        if kind == "rows":
            send, keep = products(which, (mine, theirs), after)
            tokens[event] = keep
            keeps[which], flights[which] = keep, swap(send, STEPS[which][0])
        elif kind == "add" and event[2] < 2:
            keep, came = keeps[which], flights[which]
            half = keep.shape[0] // 2
            if after:
                send, keep = kernel_call(halve_kernel, "halve", [keep, came], [floats(half, 2 * MODES)] * 2, after)
            else:
                send, keep = keep[:half] + came[:half], keep[half:] + came[half:]
            tokens[event] = keep
            keeps[which], flights[which] = keep, swap(send, STEPS[which][event[2] + 1])
        elif kind == "add":
            group = next(g for g in GROUPS if which in g)
            keep, came = keeps[which], flights[which]
            before = [groups[group]] if group in groups else []
            if after or before:
                rows = CHUNKS[which] + sum(b.shape[0] for b in before)
                (done,) = kernel_call(finish_kernel, "finish", [keep, came, *before], [floats(rows, 2 * MODES)], after)
            else:
                done = keep + came
            tokens[event] = groups[group] = done
            if which == group[-1]:
                flights[group] = lax.ppermute(done, "cuts", [(0, 1), (1, 0)])
        else:
            group = GROUPS[which]
            (table,) = kernel_call(
                functools.partial(table_kernel, sum(CHUNKS[: group[0]]), own_rows),
                "table",
                [groups[group], flights[group], table],
                [TOKEN],
                after,
            )
    for bit in (CORE, Z_NEAR, Y, Z_FAR):
        table = table + swap(table, (bit, bit))
    (values,) = kernel_call(look_up_kernel, "look_up", [table, where, scale], [floats(2, diagrams.shape[0])])
    return (jnp.concatenate([groups[g] for g in GROUPS], axis=0)[None], values.T)


def solution(mesh):
    by_halves = mesh.shape["space"] == 16 and mesh.shape["cuts"] == 2
    placed = (P("cuts", None, None, "space"), P(), P())
    return jax.shard_map(
        halving if by_halves else general,
        mesh=mesh,
        in_specs=placed,
        out_specs=(P("cuts", "space", None), P()),
        check_vma=False,
    )
```
